256 devices in a mesh: dp: 8 (over y, core), seq: 32 (over x, z).
Axes of the slice: x: 4, y: 4, z: 8, core: 2. Of those that a mesh axis runs over, the one named last changes fastest.
Arguments:
- queries: bfloat16 [32768, 4096], P(('dp', 'seq')), may hold values from -8 to 8
- keys: bfloat16 [32768, 512], P(('dp', 'seq')), may hold values from -8 to 8
- values: bfloat16 [32768, 512], P(('dp', 'seq')), may hold values from -6 to 6
- out_grad: bfloat16 [32768, 4096], P(('dp', 'seq')), may hold values from -6 to 6
- doc_lengths: int32 [64], replicated, may hold values from 1 to 1024, as said below
Outputs:
- attn_out: bfloat16 [32768, 4096], P(('dp', 'seq'))
- query_grad: bfloat16 [32768, 4096], P(('dp', 'seq'))
- gradient_keys: bfloat16 [32768, 512], P(('dp', 'seq'))
- gradient_values: bfloat16 [32768, 512], P(('dp', 'seq'))
The draws below stay inside these ranges and needn't reach their ends.
Inputs may be any that keep to these rules, and one draw needn't show every extreme that they name: `doc_lengths`: the 64 lengths sum to 32768. The documents come in 8 groups of 8, one group for each block of 4096 rows; the first of each group is 1024 rows long and starts at row 0 in the first block, exactly 512 rows before the second block, and 256 to 512 rows before every later block.
All inputs are finite; a program needn't handle non-finite values.
Results may differ from the reference program's by a relative error of at most 0.0085.
Values may be sent and summed in bfloat16 or wider, within the bound.
A program may use at most 64 MiB of HBM per device.

```python
import math
import jax
import jax.numpy as jnp
from jax import lax

QUERY_HEADS = 32
KEY_VALUE_HEADS = 4
HEAD_WIDTH = 128
DOCS_G = 8
GROUP = 4096
MOST = 1024
TOKEN_TOTAL = 32768
NDOCS = 64
N_DP = 8


def draw_queries(key, part):
    key = jax.random.fold_in(key, 1)
    return jnp.clip(jax.random.normal(key, (TOKEN_TOTAL, QUERY_HEADS * HEAD_WIDTH), jnp.float32), -6.0, 6.0).astype(jnp.bfloat16)


def draw_keys(key, part):
    key = jax.random.fold_in(key, 2)
    return jnp.clip(jax.random.normal(key, (TOKEN_TOTAL, KEY_VALUE_HEADS * HEAD_WIDTH), jnp.float32), -6.0, 6.0).astype(jnp.bfloat16)


def draw_doc_lengths(key, part):
    key = jax.random.fold_in(key, 3)
    slots = jnp.arange(N_DP)
    before = jax.random.randint(jax.random.fold_in(key, 1), (N_DP,), MOST // 4, MOST // 2 + 1)
    before = jnp.where(slots == 1, MOST // 2, before)
    before = jnp.where(slots == 0, 0, before).astype(jnp.int32)
    after = jnp.concatenate([before[1:], jnp.zeros((1,), jnp.int32)])
    rest = GROUP - after + before - MOST
    shares = jax.random.randint(jax.random.fold_in(key, 2), (N_DP, DOCS_G - 1), 2, 5)
    running = jnp.cumsum(shares, axis=1)
    ends = rest[:, None] * running // running[:, -1:]
    pieces = ends - jnp.concatenate([jnp.zeros((N_DP, 1), jnp.int32), ends[:, :-1]], axis=1)
    firsts = jnp.full((N_DP, 1), MOST, jnp.int32)
    return jnp.concatenate([firsts, pieces.astype(jnp.int32)], axis=1).reshape(NDOCS)


def shard_levels(own_key, dims, cuts, least, high):
    level, own = 1.0, jax.random.fold_in(own_key, 6)
    for axis_at, shards_of in cuts:
        steps = jnp.exp(jax.random.uniform(jax.random.fold_in(own, axis_at), (shards_of,), jnp.float32, least / len(cuts), high / len(cuts)))
        level = level * jnp.repeat(steps, dims[axis_at] // shards_of).reshape([-1 if axis == axis_at else 1 for axis in range(len(dims))])
    return level


def scatter_about(stream_key, shape, width, bound, cuts=(), kind=jnp.bfloat16):
    level = shard_levels(stream_key, shape, cuts, -0.22, 0.18) if cuts else 1.0
    values = jax.random.normal(stream_key, shape, jnp.float32) * width * level
    return jnp.minimum(jnp.maximum(values, -bound), bound).astype(kind)


def setup_inputs(seed: int = 0) -> dict:
    splits = jax.random.split(jax.random.key(seed), 6)
    return {
        "queries": draw_queries(jax.random.fold_in(splits[5], 71), 0),
        "keys": draw_keys(jax.random.fold_in(splits[5], 71), 0),
        "values": scatter_about(splits[2], (TOKEN_TOTAL, KEY_VALUE_HEADS * HEAD_WIDTH), 1.0, 6.0, ((0, 256),)),
        "out_grad": scatter_about(splits[3], (TOKEN_TOTAL, QUERY_HEADS * HEAD_WIDTH), 1.0, 6.0, ((0, 256),)),
        "doc_lengths": draw_doc_lengths(jax.random.fold_in(splits[5], 71), 0),
    }


masked_score = -1e+30

def doc_index(positions, starts):
    hits = (starts[None, :] <= positions[:, None]).astype(jnp.int32)
    return (lax.optimization_barrier(jnp.sum(hits, axis=1)) - 1).astype(jnp.int32)

def attend_block(query_block, grad_block, query_pos, query_doc, key_window, value_window, key_pos, key_doc, score_scale):
    scores = jnp.dot(query_block, key_window.T, preferred_element_type=jnp.float32) * score_scale
    allowed = (key_doc[None, :] == query_doc[:, None]) & (key_pos[None, :] <= query_pos[:, None])
    scores = jnp.where(allowed, scores, masked_score)
    highest = lax.optimization_barrier(jnp.max(scores, axis=1, keepdims=True))
    weights = jnp.where(allowed, jnp.exp(scores - highest), 0.0)
    probs = weights / lax.optimization_barrier(jnp.sum(weights, axis=1, keepdims=True))
    probs_low = probs.astype(jnp.bfloat16)
    attended = jnp.dot(probs_low, value_window, preferred_element_type=jnp.float32).astype(jnp.bfloat16)
    stored = lax.optimization_barrier(attended).astype(jnp.float32)
    delta = lax.optimization_barrier(jnp.sum(grad_block.astype(jnp.float32) * stored, axis=1, keepdims=True))
    dprobs = jnp.dot(grad_block, value_window.T, preferred_element_type=jnp.float32)
    dscores_low = (probs * (dprobs - delta)).astype(jnp.bfloat16)
    query_part = (jnp.dot(dscores_low, key_window, preferred_element_type=jnp.float32) * score_scale).astype(jnp.bfloat16)
    key_part = jnp.dot(dscores_low.T, query_block, preferred_element_type=jnp.float32) * score_scale
    value_part = jnp.dot(probs_low.T, grad_block, preferred_element_type=jnp.float32)
    return (attended, query_part, key_part, value_part)

def sweep(query_rows, grad_rows, key_rows, value_rows, key_pos, key_doc, qblock, window, score_scale):
    query_count = query_rows.shape[0]
    key_count = key_rows.shape[0]
    offset = key_count - query_count
    depth = query_rows.shape[1]
    query_pos = key_pos[offset:]
    query_doc = key_doc[offset:]

    def advance(number, totals):
        attended_all, qgrad_all, kgrad_all, vgrad_all = totals
        row_start = (number * qblock).astype(jnp.int32)
        window_start = jnp.maximum(row_start + offset + qblock - window, 0).astype(jnp.int32)
        query_block = lax.dynamic_slice_in_dim(query_rows, row_start, qblock, 0)
        grad_block = lax.dynamic_slice_in_dim(grad_rows, row_start, qblock, 0)
        block_pos = lax.dynamic_slice_in_dim(query_pos, row_start, qblock, 0)
        block_doc = lax.dynamic_slice_in_dim(query_doc, row_start, qblock, 0)
        key_window = lax.dynamic_slice_in_dim(key_rows, window_start, window, 0)
        value_window = lax.dynamic_slice_in_dim(value_rows, window_start, window, 0)
        window_pos = lax.dynamic_slice_in_dim(key_pos, window_start, window, 0)
        window_doc = lax.dynamic_slice_in_dim(key_doc, window_start, window, 0)
        attended, query_part, key_part, value_part = attend_block(query_block, grad_block, block_pos, block_doc, key_window, value_window, window_pos, window_doc, score_scale)
        attended_all = lax.dynamic_update_slice_in_dim(attended_all, attended, row_start, 0)
        qgrad_all = lax.dynamic_update_slice_in_dim(qgrad_all, query_part, row_start, 0)
        kgrad_all = lax.dynamic_update_slice_in_dim(kgrad_all, lax.dynamic_slice_in_dim(kgrad_all, window_start, window, 0) + key_part, window_start, 0)
        vgrad_all = lax.dynamic_update_slice_in_dim(vgrad_all, lax.dynamic_slice_in_dim(vgrad_all, window_start, window, 0) + value_part, window_start, 0)
        return (attended_all, qgrad_all, kgrad_all, vgrad_all)
    initial = (jnp.zeros((query_count, depth), jnp.bfloat16), jnp.zeros((query_count, depth), jnp.bfloat16), jnp.zeros((key_count, depth), jnp.float32), jnp.zeros((key_count, depth), jnp.float32))
    return lax.fori_loop(0, query_count // qblock, advance, initial)

def reference(queries, keys, values, out_grad, doc_lengths):
    group_share = QUERY_HEADS // KEY_VALUE_HEADS
    qblock = min(512, GROUP)
    window = min(qblock + MOST, TOKEN_TOTAL)
    score_scale = 1.0 / math.sqrt(HEAD_WIDTH)
    starts = (jnp.cumsum(doc_lengths) - doc_lengths).astype(jnp.int32)
    positions = jnp.arange(TOKEN_TOTAL, dtype=jnp.int32)
    documents = doc_index(positions, starts)
    query_heads = queries.reshape(TOKEN_TOTAL, QUERY_HEADS, HEAD_WIDTH).transpose(1, 0, 2)
    grad_heads = out_grad.reshape(TOKEN_TOTAL, QUERY_HEADS, HEAD_WIDTH).transpose(1, 0, 2)
    heads_of_keys = jnp.repeat(keys.reshape(TOKEN_TOTAL, KEY_VALUE_HEADS, HEAD_WIDTH).transpose(1, 0, 2), group_share, axis=0)
    heads_of_values = jnp.repeat(values.reshape(TOKEN_TOTAL, KEY_VALUE_HEADS, HEAD_WIDTH).transpose(1, 0, 2), group_share, axis=0)

    def one_head(operands):
        return sweep(operands[0], operands[1], operands[2], operands[3], positions, documents, qblock, window, score_scale)
    attended, qgrads, key_gradients, value_gradients = lax.map(one_head, (query_heads, grad_heads, heads_of_keys, heads_of_values))
    attn_out = attended.transpose(1, 0, 2).reshape(TOKEN_TOTAL, QUERY_HEADS * HEAD_WIDTH)
    query_grad = qgrads.transpose(1, 0, 2).reshape(TOKEN_TOTAL, QUERY_HEADS * HEAD_WIDTH)
    gradient_keys = lax.optimization_barrier(jnp.sum(key_gradients.reshape(KEY_VALUE_HEADS, group_share, TOKEN_TOTAL, HEAD_WIDTH), axis=1)).transpose(1, 0, 2).reshape(TOKEN_TOTAL, KEY_VALUE_HEADS * HEAD_WIDTH).astype(jnp.bfloat16)
    gradient_values = lax.optimization_barrier(jnp.sum(value_gradients.reshape(KEY_VALUE_HEADS, group_share, TOKEN_TOTAL, HEAD_WIDTH), axis=1)).transpose(1, 0, 2).reshape(TOKEN_TOTAL, KEY_VALUE_HEADS * HEAD_WIDTH).astype(jnp.bfloat16)
    return (attn_out, query_grad, gradient_keys, gradient_values)
```

```python
import functools
import math

import jax
import jax.numpy as jnp
from jax import lax
from jax.experimental import pallas as pl
from jax.experimental.pallas import tpu as pltpu
from jax.sharding import PartitionSpec as P

MESH = pl.DeviceIdType.MESH
WIDTH = 128
REACH = 8
FORWARD = 4
MASKED = -1e30
BF16 = jnp.bfloat16
F32 = jnp.float32


def nt(a, b):
    return lax.dot_general(a, b, (((1,), (1,)), ((), ())), preferred_element_type=F32)


def nn(a, b):
    return lax.dot_general(a, b, (((1,), (0,)), ((), ())), preferred_element_type=F32)


def kernel(
    dims,
    lengths,
    queries,
    keys,
    values,
    out_grad,
    attended,
    query_grad,
    key_grad,
    value_grad,
    q_s,
    do_s,
    kv_s,
    o_s,
    dq_s,
    bias_s,
    t_s,
    dp_s,
    p_s,
    ds_s,
    part_s,
    own_s,
    back_s,
    fin_s,
    load_sem,
    store_sem,
    in_send,
    in_recv,
    out_send,
    out_recv,
):
    n_dp, n_seq, rows, heads, kv_heads = dims
    share = heads // kv_heads
    blocks = REACH + 1
    span = blocks * rows
    total = n_dp * n_seq
    scale = 1.0 / math.sqrt(WIDTH)
    me = lax.axis_index("dp") * n_seq + lax.axis_index("seq")

    def device(distance):
        flat = lax.rem(me + (distance + total), total)
        return (flat // n_seq, lax.rem(flat, n_seq))

    after, before, far_after, far_before = device(1), device(-1), device(REACH), device(-REACH)

    def own_kv(g):
        cols = pl.ds(g * WIDTH, WIDTH)
        return (
            pltpu.make_async_copy(keys.at[:, cols], kv_s.at[g, REACH, 0], load_sem.at[2 * heads + 2 * g]),
            pltpu.make_async_copy(
                values.at[:, cols], kv_s.at[g, REACH, 1], load_sem.at[2 * heads + 2 * g + 1]
            ),
        )

    def own_q(h):
        cols = pl.ds(pl.multiple_of(h * WIDTH, WIDTH), WIDTH)
        to = pl.ds(pl.multiple_of(h * rows, rows), rows)
        return (
            pltpu.make_async_copy(queries.at[:, cols], q_s.at[to], load_sem.at[2 * h]),
            pltpu.make_async_copy(out_grad.at[:, cols], do_s.at[to], load_sem.at[2 * h + 1]),
        )

    for g in range(kv_heads):
        for copy in own_kv(g):
            copy.start()

    @pl.loop(0, heads)
    def _(h):
        for copy in own_q(h):
            copy.start()

    barrier = pltpu.get_barrier_semaphore()
    for peer in (after, before, far_after, far_before):
        pl.semaphore_signal(barrier, inc=1, device_id=peer, device_id_type=MESH)
    pl.semaphore_wait(barrier, 4)

    def hand(g, k, to, peer, send):
        return pltpu.make_async_remote_copy(
            src_ref=kv_s.at[g, REACH - k],
            dst_ref=kv_s.at[g, REACH - to],
            send_sem=in_send.at[g, send],
            recv_sem=in_recv.at[g, to],
            device_id=peer,
            device_id_type=MESH,
        )

    def give_first(g):
        return hand(g, 0, REACH, far_after, REACH + 1)

    def give_up(g, k):
        return hand(g, k, k + 1, after, k)

    def give_down(g, k):
        return hand(g, k, k - 1, before, k)

    for g in range(kv_heads):
        for copy in own_kv(g):
            copy.wait()
        give_up(g, 0).start()
        give_first(g).start()

    row_pos = me * rows + lax.broadcasted_iota(jnp.int32, (1, rows), 1)

    def find(d, carry):
        start, cum = carry
        return jnp.where(row_pos >= cum, cum, start), cum + lengths[d]

    doc_start, _ = lax.fori_loop(
        0, lengths.shape[0], find, (jnp.zeros((1, rows), jnp.int32), jnp.int32(0))
    )
    for b in range(blocks):
        key_pos = (me + (b - REACH)) * rows + lax.broadcasted_iota(jnp.int32, (rows, rows), 0)
        allowed = (key_pos >= doc_start) & (key_pos <= row_pos)
        bias_s[b * rows : (b + 1) * rows, :] = jnp.where(allowed, 0.0, MASKED)

    order = sorted(
        ((s, g) for s in range(1, FORWARD) for g in range(kv_heads)), key=lambda sg: sg[0] * 2.3 + sg[1]
    )
    for s, g in order:
        give_first(g).wait_recv() if s == 1 else give_down(g, REACH + 2 - s).wait_recv()
        give_down(g, REACH + 1 - s).start()
        give_up(g, s - 1).wait_recv()
        give_up(g, s).start()

    @pl.loop(0, heads)
    def _(h):
        for copy in own_q(h):
            copy.wait()

    def back(g, way, k, to, peer):
        return pltpu.make_async_remote_copy(
            src_ref=part_s.at[g, k],
            dst_ref=back_s.at[g, way, to],
            send_sem=out_send.at[g, k],
            recv_sem=out_recv.at[g, way, to],
            device_id=peer,
            device_id_type=MESH,
        )

    def back_down(g, k):
        return back(g, 0, k, k - 1, before)

    def back_up(g, k):
        return back(g, 1, k, k + 1, after) if k < REACH else back(g, 1, k, 0, far_before)

    def stage(g, s):
        low, high = FORWARD - s, FORWARD + 1 + s
        if s:
            back_down(g, low + 1).wait_recv()
            part_s[g, low] = (part_s[g, low].astype(F32) + back_s[g, 0, low].astype(F32)).astype(BF16)
        back_down(g, low).start()
        if s:
            back_up(g, high - 1).wait_recv()
            part_s[g, high] = (part_s[g, high].astype(F32) + back_s[g, 1, high].astype(F32)).astype(BF16)
        back_up(g, high).start()

    def last_stage(g):
        back_down(g, 1).wait_recv()
        back_up(g, REACH).wait_recv()
        total_kv = own_s[g] + back_s[g, 0, 0].astype(F32) + back_s[g, 1, 0].astype(F32)
        cols = pl.ds(pl.multiple_of(g * WIDTH, WIDTH), WIDTH)
        fin_s[0, :, cols] = total_kv[0].astype(BF16)
        fin_s[1, :, cols] = total_kv[1].astype(BF16)

    factor = scale * math.log2(math.e)

    def compute(g):
        k_all = kv_s[g, :, 0].reshape(span, WIDTH)
        v_all = kv_s[g, :, 1].reshape(span, WIDTH)
        for pair in range(share // 2):
            slot = pair % 2
            at = pl.ds(pl.multiple_of(g * (share * rows) + pair * 2 * rows, 2 * rows), 2 * rows)
            q_pair, do_pair = q_s[at], do_s[at]
            cols = slice(pair * 2 * rows, (pair + 1) * 2 * rows)
            high = jnp.full((8, 2 * rows), MASKED, F32)
            for b in range(blocks):
                r = slice(b * rows, (b + 1) * rows)
                bias = bias_s[r, :]
                t = nt(kv_s[g, b, 0], q_pair) * factor + jnp.concatenate([bias, bias], axis=1)
                t_s[slot, r, :] = t
                high = jnp.maximum(high, jnp.max(t.reshape(rows // 8, 8, 2 * rows), axis=0))
            high = jnp.max(high, axis=0, keepdims=True)
            norm = jnp.zeros((8, 2 * rows), F32)
            mix = jnp.zeros((8, 2 * rows), F32)
            for b in range(blocks):
                r = slice(b * rows, (b + 1) * rows)
                w = jnp.exp2(t_s[slot, r, :] - high)
                dp = nt(kv_s[g, b, 1], do_pair)
                t_s[slot, r, :] = w
                dp_s[slot, r, :] = dp
                norm += jnp.sum(w.reshape(rows // 8, 8, 2 * rows), axis=0)
                mix += jnp.sum((w * dp).reshape(rows // 8, 8, 2 * rows), axis=0)
            inverse = 1.0 / jnp.sum(norm, axis=0, keepdims=True)
            delta = jnp.sum(mix, axis=0, keepdims=True) * inverse
            for b in range(blocks):
                r = slice(b * rows, (b + 1) * rows)
                p = t_s[slot, r, :] * inverse
                p_s[r, cols] = p.astype(BF16)
                ds_s[r, cols] = (p * (dp_s[slot, r, :] - delta)).astype(BF16)
        at = pl.ds(pl.multiple_of(g * (share * rows), share * rows), share * rows)
        dv = nn(p_s[...], do_s[at]).reshape(blocks, rows, WIDTH)
        dk = (nn(ds_s[...], q_s[at]) * scale).reshape(blocks, rows, WIDTH)
        own_s[g, 0] = dk[REACH]
        own_s[g, 1] = dv[REACH]
        for k in range(1, blocks):
            part_s[g, k, 0] = dk[REACH - k].astype(BF16)
            part_s[g, k, 1] = dv[REACH - k].astype(BF16)
        o_t = nn(v_all.T, p_s[...])
        dq_t = nn(k_all.T, ds_s[...]) * scale
        for h in range(share):
            cols = pl.ds(pl.multiple_of((g * share + h) * WIDTH, WIDTH), WIDTH)
            r = slice(h * rows, (h + 1) * rows)
            o_s[:, cols] = o_t[:, r].T.astype(BF16)
            dq_s[:, cols] = dq_t[:, r].T.astype(BF16)

    def store_heads(g):
        cols = pl.ds(pl.multiple_of(g * (share * WIDTH), share * WIDTH), share * WIDTH)
        return (
            pltpu.make_async_copy(o_s.at[:, cols], attended.at[:, cols], store_sem.at[2 * g]),
            pltpu.make_async_copy(dq_s.at[:, cols], query_grad.at[:, cols], store_sem.at[2 * g + 1]),
        )

    @pl.loop(0, kv_heads)
    def _(g):
        give_up(g, FORWARD - 1).wait_recv()
        give_down(g, FORWARD + 2).wait_recv()
        compute(g)
        stage(g, 0)
        for copy in store_heads(g):
            copy.start()
        for s in range(1, FORWARD):

            @pl.when(g >= s)
            def _():
                stage(g - s, s)

    for late in range(1, FORWARD):
        for s in range(late, FORWARD):
            stage(kv_heads - 1 + late - s, s)
    for g in range(kv_heads):
        last_stage(g)

    finals = (
        pltpu.make_async_copy(fin_s.at[0], key_grad, store_sem.at[2 * kv_heads]),
        pltpu.make_async_copy(fin_s.at[1], value_grad, store_sem.at[2 * kv_heads + 1]),
    )
    for copy in finals:
        copy.start()
    for g in range(kv_heads):
        give_first(g).wait_send()
        for k in range(FORWARD):
            give_up(g, k).wait_send()
        for k in range(FORWARD + 2, REACH + 1):
            give_down(g, k).wait_send()
        for s in range(FORWARD):
            back_down(g, FORWARD - s).wait_send()
            back_up(g, FORWARD + 1 + s).wait_send()
        for copy in store_heads(g):
            copy.wait()
    for copy in finals:
        copy.wait()


def per_device(queries, keys, values, out_grad, doc_lengths):
    rows, columns = queries.shape
    heads, kv_heads = columns // WIDTH, keys.shape[1] // WIDTH
    share = heads // kv_heads
    blocks = REACH + 1
    span = blocks * rows
    dims = (lax.axis_size("dp"), lax.axis_size("seq"), rows, heads, kv_heads)
    hbm = pl.BlockSpec(memory_space=pl.ANY)
    vmem = pltpu.VMEM
    return pl.pallas_call(
        functools.partial(kernel, dims),
        out_shape=tuple(jax.ShapeDtypeStruct(a.shape, BF16) for a in (queries, queries, keys, values)),
        in_specs=[pl.BlockSpec(memory_space=pltpu.SMEM)] + [hbm] * 4,
        out_specs=[hbm] * 4,
        scratch_shapes=[
            vmem((heads * rows, WIDTH), BF16),
            vmem((heads * rows, WIDTH), BF16),
            vmem((kv_heads, blocks, 2, rows, WIDTH), BF16),
            vmem((rows, columns), BF16),
            vmem((rows, columns), BF16),
            vmem((span, rows), F32),
            vmem((2, span, 2 * rows), F32),
            vmem((2, span, 2 * rows), F32),
            vmem((span, share * rows), BF16),
            vmem((span, share * rows), BF16),
            vmem((kv_heads, blocks, 2, rows, WIDTH), BF16),
            vmem((kv_heads, 2, rows, WIDTH), F32),
            vmem((kv_heads, 2, blocks, 2, rows, WIDTH), BF16),
            vmem((2, rows, kv_heads * WIDTH), BF16),
            pltpu.SemaphoreType.DMA((2 * heads + 2 * kv_heads,)),
            pltpu.SemaphoreType.DMA((2 * kv_heads + 2,)),
            pltpu.SemaphoreType.DMA((kv_heads, REACH + 2)),
            pltpu.SemaphoreType.DMA((kv_heads, REACH + 1)),
            pltpu.SemaphoreType.DMA((kv_heads, REACH + 1)),
            pltpu.SemaphoreType.DMA((kv_heads, 2, REACH + 1)),
        ],
        compiler_params=pltpu.CompilerParams(
            collective_id=0, has_side_effects=True, vmem_limit_bytes=56 * 1024 * 1024
        ),
    )(doc_lengths, queries, keys, values, out_grad)


def solution(mesh):
    split = P(("dp", "seq"), None)
    return jax.shard_map(
        per_device,
        mesh=mesh,
        in_specs=(split, split, split, split, P()),
        out_specs=(split, split, split, split),
        check_vma=False,
    )
```
